512 devices in a mesh: layer: 4 (over y_lo, core), dp: 128 (over z, x, y_hi).
Axes of the slice: x: 4, y: 8 (y_hi: 4, y_lo: 2; y = y_hi * 2 + y_lo), z: 8, core: 2. Of those that a mesh axis runs over, the one named last changes fastest.
Arguments:
- activations: bfloat16 [4, 16384, 5120], P('layer', 'dp'), may hold values from -6 to 6
- out_grads: bfloat16 [4, 16384, 5120], P('layer', 'dp'), may hold values from -6 to 6
- projectors: bfloat16 [4, 5120, 128], P('layer'), may hold values from -0.078125 to 0.078125
- rewards: float32 [512], P('dp'), may hold values from -8 to 8
- lengths: int32 [512], P('dp'), may hold values from 1 to 32, 12288 in all
- pairing: int32 [256, 2], P('dp'), may hold values from 0 to 3, as said below
- queries: bfloat16 [4, 1024, 4096], P('layer', 'dp'), may hold values from -0.0078125 to 0.0078125
Outputs:
- scores: float32 [256, 1024], P('dp', 'layer')
The draws below stay inside these ranges and needn't reach their ends.
Inputs may be any that keep to these rules, and one draw needn't show every extreme that they name: `pairing`: the 2 pairs of one dp index name each of that index's 2 * 2 sequences exactly once.
All inputs are finite; a program needn't handle non-finite values. No bound on the sum of `lengths` on one device may be relied on, other than what follows from the above.
Results may differ from the reference program's by a relative error of at most 0.0029.
Values may be sent and summed in bfloat16 or wider, within the bound.
No kernel may reach another device: no remote copies, remote signals or barrier semaphores. Data moves between devices by JAX's collectives and lax.ppermute only.
A program may use at most 64 MiB of HBM per device.

```python
import math
import jax
import jax.numpy as jnp
import numpy as np
from jax import lax

D = 5120
K = 64
PAIR_DEV = 2
LEN = 32
PROJS = 4
PAIRS = 256
SEQS = 512
TOKENS = 16384
QUERIES = 1024


def draw_pairing(key, part):
    key = jax.random.fold_in(key, 11)
    blocks = PAIRS // PAIR_DEV
    subkeys = jax.random.split(key, blocks)
    orders = jax.vmap(lambda subkey: jax.random.permutation(subkey, 2 * PAIR_DEV))(subkeys)
    return orders.reshape(PAIRS, 2).astype(jnp.int32)


def levels(stream_key, extent, cuts, least, high):
    gain = 1.0
    for dim, shards_of in cuts:
        draws = jax.random.uniform(jax.random.fold_in(jax.random.fold_in(stream_key, 6), dim), (shards_of,), jnp.float32, least / len(cuts), high / len(cuts))
        gain = gain * jnp.repeat(jnp.exp(draws), extent[dim] // shards_of).reshape((-1,) + (1,) * (len(extent) - 1 - dim))
    return gain


def profile(number_of, total, reach, slope):
    portions = [(1 << 20) // math.isqrt(rank ** slope) + 1 for rank in range(2, number_of + 1)]
    rest, given = total - reach - (number_of - 1), [1] * (number_of - 1)
    while rest > 0:
        free = [i for i in range(number_of - 1) if given[i] < reach]
        pool, remaining = sum([portions[i] for i in free]), rest
        for i in free:
            extra = min(reach - given[i], max(1, remaining * portions[i] // pool), rest)
            given[i] = given[i] + extra
            rest = rest - extra
    return np.array([reach] + given)


def ragged_sizes(own_key, amount, total, most, slope):
    if amount == 2:
        one = jax.random.randint(own_key, (), max(1, total - most), min(most, total - 1) + 1)
        return jnp.stack([one, total - one])
    sizes = jnp.asarray(profile(amount, total, most, slope), jnp.int32)
    pairs = (amount - 1) // 2
    source_of, receiver = sizes[1:1 + 2 * pairs:2], sizes[2:2 + 2 * pairs:2]
    room = jnp.minimum(source_of - 1, most - receiver)
    shifted = jax.random.randint(jax.random.fold_in(own_key, 1), (pairs,), 0, 1 << 20) % (room + 1)
    sizes = sizes.at[1:1 + 2 * pairs:2].set(source_of - shifted).at[2:2 + 2 * pairs:2].set(receiver + shifted)
    return sizes[jax.random.permutation(jax.random.fold_in(own_key, 2), amount)]


def noise(key, shape, spread, limit, pieces=(), kind=jnp.bfloat16):
    loudness = levels(key, shape, pieces, -0.22, 0.18) if pieces else 1.0
    result = jax.random.normal(key, shape, jnp.float32) * spread * loudness
    return jnp.minimum(jnp.maximum(result, -limit), limit).astype(kind)


def setup_inputs(seed: int = 0) -> dict:
    seeds = jax.random.split(jax.random.key(seed), 8)
    return {
        "activations": noise(seeds[0], (PROJS, TOKENS, D), 1.0, 6.0, ((0, 4), (1, 128))),
        "out_grads": noise(seeds[1], (PROJS, TOKENS, D), 1.0, 6.0, ((0, 4), (1, 128))),
        "projectors": noise(seeds[2], (PROJS, D, 2 * K), D ** -0.5, 0.078125, ((0, 4),)),
        "rewards": noise(seeds[3], (SEQS,), 2.0, 8.0, ((0, 128),), jnp.float32),
        "lengths": ragged_sizes(seeds[4], SEQS, (3 * SEQS * LEN) // 4, LEN, 1).astype(jnp.int32),
        "pairing": draw_pairing(jax.random.fold_in(seeds[7], 71), 0),
        "queries": noise(seeds[6], (PROJS, QUERIES, K * K), (4 * K * K * LEN) ** -0.5, 0.0078125, ((0, 4), (1, 128))),
    }


def reference(activations, out_grads, projectors, rewards, lengths, pairing, queries):
    places = jnp.arange(LEN, dtype=jnp.int32)
    live_mask = (places[None, :] < lengths[:, None]).astype(jnp.float32)
    offsets = (jnp.arange(PAIRS, dtype=jnp.int32) // PAIR_DEV) * (2 * PAIR_DEV)
    chosen = offsets + pairing[:, 0]
    rejected = offsets + pairing[:, 1]
    margin_weight = 1.0 - jax.nn.sigmoid(rewards[chosen] - rewards[rejected])
    scores = jnp.zeros((PAIRS, QUERIES), jnp.float32)
    for index in range(projectors.shape[0]):
        proj_act = jnp.dot(activations[index], projectors[index, :, :K], preferred_element_type=jnp.float32)
        proj_grad = jnp.dot(out_grads[index], projectors[index, :, K:], preferred_element_type=jnp.float32)
        grad_rows = proj_grad.reshape(SEQS, LEN, K) * live_mask[:, :, None]
        act_rows = proj_act.reshape(SEQS, LEN, K)
        seq_grads = jnp.einsum("stk,stj->skj", grad_rows, act_rows, precision=lax.Precision.HIGHEST).reshape(SEQS, K * K)
        train_grads = (margin_weight[:, None] * (seq_grads[rejected] - seq_grads[chosen])).astype(jnp.bfloat16)
        scores = scores + jnp.dot(train_grads, queries[index].T, preferred_element_type=jnp.float32)
    return scores
```

```python
import jax
import jax.numpy as jnp
from jax import lax
from jax.experimental import pallas as pl
from jax.experimental.pallas import tpu as pltpu
from jax.sharding import Mesh, PartitionSpec as P

DP = ("zh", "zl", "x", "yhh", "yhl")
PAIR_AXES = ("zl", "x", "yhh")
QUERY_AXES = ("zh", "yhl")
CHUNKS = 4
F32 = jnp.float32
BF16 = jnp.bfloat16


def train_kernel(act, grad, proj, rewards, lengths, pairing, out, rows_v, proj_v, outer, sems):
    tokens, width = act.shape[1], act.shape[2]
    step = width // CHUNKS
    copies = []
    for i in range(CHUNKS):
        cols = pl.ds(i * step, step)
        copies.append([
            pltpu.make_async_copy(act.at[0, :, cols], rows_v.at[pl.ds(0, tokens), cols], sems.at[i, 0]),
            pltpu.make_async_copy(grad.at[0, :, cols], rows_v.at[pl.ds(tokens, tokens), cols], sems.at[i, 1]),
            pltpu.make_async_copy(proj.at[0, cols, :], proj_v.at[cols, :], sems.at[i, 2]),
        ])
        for c in copies[-1]:
            c.start()
    half = proj.shape[2] // 2
    seqs = lengths.shape[0]
    slots = tokens // seqs
    pairs = pairing.shape[0]
    place = lax.broadcasted_iota(jnp.int32, (slots, half), 0)
    signs, weights = [], []
    for p in range(pairs):
        chosen, rejected = pairing[p, 0], pairing[p, 1]
        blocks = []
        margin = jnp.float32(0)
        for s in range(seqs):
            coef = jnp.where(rejected == s, 1.0, 0.0) - jnp.where(chosen == s, 1.0, 0.0)
            blocks.append(jnp.where(place < lengths[s], coef, 0.0))
            margin = jnp.where(chosen == s, margin + rewards[s], margin)
        for s in range(seqs):
            margin = jnp.where(rejected == s, margin - rewards[s], margin)
        signs.append(jnp.concatenate(blocks, axis=0))
        weights.append(1.0 - jax.nn.sigmoid(jnp.full((half, half), margin, F32)))
    total = jnp.zeros((2 * tokens, 2 * half), F32)
    for i in range(CHUNKS):
        for c in copies[i]:
            c.wait()
        cols = pl.ds(i * step, step)
        total += jnp.dot(rows_v[:, cols], proj_v[cols, :], preferred_element_type=F32)
    a = total[:tokens, :half]
    g = total[tokens:, half:]
    g = jnp.concatenate([g * s for s in signs], axis=1)
    g_hi = g.astype(BF16)
    g_lo = (g - g_hi.astype(F32)).astype(BF16)
    a_hi = a.astype(BF16)
    a_lo = (a - a_hi.astype(F32)).astype(BF16)

    def over_tokens(l, r):
        return lax.dot_general(l, r, (((0,), (0,)), ((), ())), preferred_element_type=F32)

    t = over_tokens(g_hi, a_hi) + (over_tokens(g_hi, a_lo) + over_tokens(g_lo, a_hi))
    outer[:, :half] = t * jnp.concatenate(weights, axis=0)
    parts = [outer[pl.ds(k, pairs * 8, stride=8), :half] for k in range(8)]
    flat = jnp.concatenate(parts, axis=1).astype(BF16)
    for n in range(out.shape[0]):
        out[n] = flat


def score_kernel(train, queries, out, train_f):
    members = train.shape[0]
    group = lax.axis_index("x")
    span = queries.shape[0] // 4
    for name in PAIR_AXES[2:]:
        group = group * lax.axis_size(name) + lax.axis_index(name)
    for j in range(4):
        train_f[j] = train[:, :, 128 * j : 128 * j + 128].reshape(train_f.shape[1:]).astype(F32)
    total = None
    for s in range(8):
        rows = [train_f[j, pl.ds(s, members * 2, stride=8), :].astype(BF16) for j in range(4)]
        rows = jnp.concatenate(rows, axis=1)
        term = lax.dot_general(
            rows, queries[:, pl.ds(512 * s, 512)], (((1,), (1,)), ((), ())), preferred_element_type=F32
        )
        total = term if total is None else total + term
    if total.shape[1] < 128:
        total = jnp.concatenate([total, jnp.zeros((total.shape[0], 128 - total.shape[1]), F32)], axis=1)
    lane = lax.broadcasted_iota(jnp.int32, total.shape, 1)
    for layer in range(4):
        mine = jnp.where(lane // span == layer, total, 0.0)
        shift = lax.rem(group * span + (128 - layer * span), 128)
        out[layer] = pltpu.roll(mine, shift, 1)


def sum_kernel(got, out):
    terms = got[...]
    group = got.shape[0] // 8
    for half in range(2):
        total = None
        for layer in range(4):
            for k in range(group):
                term = terms[(layer * 2 + half) * group + k]
                total = term if total is None else total + term
        out[:, 128 * half : 128 * half + 128] = total


def local(activations, out_grads, projectors, rewards, lengths, pairing, queries):
    tokens, width = activations.shape[1:]
    members = lax.axis_size(PAIR_AXES)
    holders = lax.axis_size(QUERY_AXES)
    hbm = pl.BlockSpec(memory_space=pltpu.HBM)
    smem = pl.BlockSpec(memory_space=pltpu.SMEM)
    vmem = pl.BlockSpec(memory_space=pltpu.VMEM)

    sent_queries = jnp.broadcast_to(queries, (holders,) + queries.shape[1:])
    held = lax.all_to_all(sent_queries, QUERY_AXES, 0, 0).reshape(-1, queries.shape[2])

    sent = pl.pallas_call(
        train_kernel,
        out_shape=jax.ShapeDtypeStruct((members, 16, 512), BF16),
        in_specs=[hbm, hbm, hbm, smem, smem, smem],
        out_specs=vmem,
        scratch_shapes=[
            pltpu.VMEM((2 * tokens, width), BF16),
            pltpu.VMEM((width, projectors.shape[2]), BF16),
            pltpu.VMEM((projectors.shape[2], projectors.shape[2]), F32),
            pltpu.SemaphoreType.DMA((CHUNKS, 3)),
        ],
        compiler_params=pltpu.CompilerParams(vmem_limit_bytes=60 << 20),
        cost_estimate=pl.CostEstimate(flops=8 * 256 * 5120 * 128, bytes_accessed=32 << 20, transcendentals=0),
        name="train",
    )(activations, out_grads, projectors, rewards, lengths, pairing)
    gathered = lax.all_to_all(sent, PAIR_AXES, 0, 0)

    partial = pl.pallas_call(
        score_kernel,
        out_shape=jax.ShapeDtypeStruct((4, members * 2, 128), F32),
        in_specs=[vmem, vmem],
        out_specs=vmem,
        scratch_shapes=[pltpu.VMEM((4, members * 16, 128), F32)],
        compiler_params=pltpu.CompilerParams(vmem_limit_bytes=16 << 20),
        cost_estimate=pl.CostEstimate(flops=2 * 32 * 64 * 4096, bytes_accessed=1 << 20, transcendentals=0),
        name="score",
    )(gathered, held)
    got = lax.all_to_all(partial.reshape(4 * members, 2, 128), ("layer",) + PAIR_AXES, 0, 0)
    return pl.pallas_call(
        sum_kernel,
        out_shape=jax.ShapeDtypeStruct((2, 256), F32),
        in_specs=[vmem],
        out_specs=vmem,
        name="total",
    )(got)


def solution(mesh):
    fine = Mesh(mesh.devices.reshape(4, 4, 2, 4, 2, 2), ("layer",) + DP)
    return jax.shard_map(
        local,
        mesh=fine,
        in_specs=(
            P("layer", DP, None),
            P("layer", DP, None),
            P("layer", None, None),
            P(DP),
            P(DP),
            P(DP, None),
            P("layer", DP, None),
        ),
        out_specs=P(DP, "layer"),
        check_vma=False,
    )
```

```python
import jax
import jax.numpy as jnp
from jax import lax
from jax.experimental import pallas as pl
from jax.experimental.pallas import tpu as pltpu
from jax.sharding import Mesh, PartitionSpec as P

DP = ("zh", "zm", "zl", "x", "yh")
PAIR_AXES = ("zl", "zm", "zh")
QUERY_AXES = (("yh",), ("x",))
CHUNKS = 4
F32 = jnp.float32
BF16 = jnp.bfloat16


def train_kernel(act, grad, proj, rewards, lengths, pairing, out, rows_v, proj_v, outer, sems):
    tokens, width = act.shape[1], act.shape[2]
    step = width // CHUNKS
    copies = []
    for i in range(CHUNKS):
        cols = pl.ds(i * step, step)
        copies.append([
            pltpu.make_async_copy(act.at[0, :, cols], rows_v.at[pl.ds(0, tokens), cols], sems.at[i, 0]),
            pltpu.make_async_copy(grad.at[0, :, cols], rows_v.at[pl.ds(tokens, tokens), cols], sems.at[i, 1]),
            pltpu.make_async_copy(proj.at[0, cols, :], proj_v.at[cols, :], sems.at[i, 2]),
        ])
        for c in copies[-1]:
            c.start()
    half = proj.shape[2] // 2
    seqs = lengths.shape[0]
    slots = tokens // seqs
    pairs = pairing.shape[0]
    place = lax.broadcasted_iota(jnp.int32, (slots, half), 0)
    signs, weights = [], []
    for p in range(pairs):
        chosen, rejected = pairing[p, 0], pairing[p, 1]
        blocks = []
        margin = jnp.float32(0)
        for s in range(seqs):
            coef = jnp.where(rejected == s, 1.0, 0.0) - jnp.where(chosen == s, 1.0, 0.0)
            blocks.append(jnp.where(place < lengths[s], coef, 0.0))
            margin = jnp.where(chosen == s, margin + rewards[s], margin)
        for s in range(seqs):
            margin = jnp.where(rejected == s, margin - rewards[s], margin)
        signs.append(jnp.concatenate(blocks, axis=0))
        weights.append(1.0 - jax.nn.sigmoid(jnp.full((half, half), margin, F32)))
    total = jnp.zeros((2 * tokens, 2 * half), F32)
    for i in range(CHUNKS):
        for c in copies[i]:
            c.wait()
        cols = pl.ds(i * step, step)
        total += jnp.dot(rows_v[:, cols], proj_v[cols, :], preferred_element_type=F32)
    a = total[:tokens, :half]
    g = total[tokens:, half:]
    g = jnp.concatenate([g * s for s in signs], axis=1)
    g_hi = g.astype(BF16)
    g_lo = (g - g_hi.astype(F32)).astype(BF16)
    a_hi = a.astype(BF16)
    a_lo = (a - a_hi.astype(F32)).astype(BF16)

    def over_tokens(l, r):
        return lax.dot_general(l, r, (((0,), (0,)), ((), ())), preferred_element_type=F32)

    t = over_tokens(g_hi, a_hi) + (over_tokens(g_hi, a_lo) + over_tokens(g_lo, a_hi))
    outer[:, :half] = t * jnp.concatenate(weights, axis=0)
    parts = [outer[pl.ds(k, pairs * 8, stride=8), :half] for k in range(8)]
    flat = jnp.concatenate(parts, axis=1).astype(BF16)
    out[...] = flat


def score_kernel(train, queries, out, train_f):
    members = train.shape[0] // 16
    for j in range(4):
        train_f[j] = train[:, 128 * j : 128 * j + 128].astype(F32)
    total = None
    for s in range(8):
        rows = [train_f[j, pl.ds(s, members * 2, stride=8), :].astype(BF16) for j in range(4)]
        rows = jnp.concatenate(rows, axis=1)
        term = lax.dot_general(
            rows, queries[:, pl.ds(512 * s, 512)], (((1,), (1,)), ((), ())), preferred_element_type=F32
        )
        total = term if total is None else total + term
    mine = lax.axis_index("zh") * 2 + lax.axis_index("zm")
    for layer in range(4):
        out[layer] = jnp.where(mine == layer, total, 0.0)


def sum_kernel(got, out):
    for half in range(2):
        total = got[0, half]
        for k in range(1, got.shape[0]):
            total = total + got[k, half]
        out[:, 128 * half : 128 * half + 128] = total


def local(activations, out_grads, projectors, rewards, lengths, pairing, queries):
    tokens, width = activations.shape[1:]
    members = lax.axis_size(PAIR_AXES)
    hbm = pl.BlockSpec(memory_space=pltpu.HBM)
    smem = pl.BlockSpec(memory_space=pltpu.SMEM)
    vmem = pl.BlockSpec(memory_space=pltpu.VMEM)

    train = pl.pallas_call(
        train_kernel,
        out_shape=jax.ShapeDtypeStruct((16, 512), BF16),
        in_specs=[hbm, hbm, hbm, smem, smem, smem],
        out_specs=vmem,
        scratch_shapes=[
            pltpu.VMEM((2 * tokens, width), BF16),
            pltpu.VMEM((width, projectors.shape[2]), BF16),
            pltpu.VMEM((projectors.shape[2], projectors.shape[2]), F32),
            pltpu.SemaphoreType.DMA((CHUNKS, 3)),
        ],
        compiler_params=pltpu.CompilerParams(vmem_limit_bytes=62200000),
        cost_estimate=pl.CostEstimate(flops=2 * 256 * 5120 * 128, bytes_accessed=4 << 20, transcendentals=0),
        name="train",
    )(activations, out_grads, projectors, rewards, lengths, pairing)
    held = queries[0]
    gathers = list(PAIR_AXES)
    for stage, axes in enumerate(QUERY_AXES):
        copies = jnp.broadcast_to(held, (lax.axis_size(axes),) + held.shape)
        held = lax.all_to_all(copies, axes, 0, 0).reshape(-1, held.shape[1])
        if stage == 0:
            for axis in gathers[:1]:
                train = lax.all_gather(train, axis, axis=0, tiled=True)
            held, train = lax.optimization_barrier((held, train))
    for axis in gathers[1:]:
        train = lax.all_gather(train, axis, axis=0, tiled=True)

    partial = pl.pallas_call(
        score_kernel,
        out_shape=jax.ShapeDtypeStruct((4, members * 2, 128), F32),
        in_specs=[vmem, vmem],
        out_specs=vmem,
        scratch_shapes=[pltpu.VMEM((4, members * 16, 128), F32)],
        compiler_params=pltpu.CompilerParams(vmem_limit_bytes=16 << 20),
        cost_estimate=pl.CostEstimate(flops=2 * 32 * 64 * 4096, bytes_accessed=1 << 20, transcendentals=0),
        name="score",
    )(train, held)
    got = lax.all_to_all(partial.reshape(4 * members, 2, 128), ("layer", "zh", "zm", "zl"), 0, 0)
    return pl.pallas_call(
        sum_kernel,
        out_shape=jax.ShapeDtypeStruct((2, 256), F32),
        in_specs=[vmem],
        out_specs=vmem,
        compiler_params=pltpu.CompilerParams(vmem_limit_bytes=1 << 20),
        name="total",
    )(got.reshape(-1, 2, 2, 128))


def solution(mesh):
    fine = Mesh(mesh.devices.reshape(4, 2, 2, 2, 4, 4), ("layer",) + DP)
    return jax.shard_map(
        local,
        mesh=fine,
        in_specs=(
            P("layer", DP, None),
            P("layer", DP, None),
            P("layer", None, None),
            P(DP),
            P(DP),
            P(DP, None),
            P("layer", DP, None),
        ),
        out_specs=P(DP, "layer"),
        check_vma=False,
    )
```

```python
import jax
import jax.numpy as jnp
from jax import lax
from jax.experimental import pallas as pl
from jax.experimental.pallas import tpu as pltpu
from jax.sharding import Mesh, PartitionSpec as P

DP = ("zh", "zm", "zl", "x", "yh")
PAIR_AXES = ("zl", "zm", "zh")
QUERY_AXES = (("yh",), ("x",))
CHUNKS = 4
F32 = jnp.float32
BF16 = jnp.bfloat16


def train_kernel(
    act, grad, proj, rewards_in, lengths_in, pairing_in, out, rows_v, proj_v, outer, rewards, lengths, pairing, sems, small
):
    given = [(rewards_in, rewards), (lengths_in, lengths), (pairing_in, pairing)]
    scalars = [pltpu.make_async_copy(a, b, small.at[i]) for i, (a, b) in enumerate(given)]
    for c in scalars:
        c.start()
    tokens, width = act.shape[1], act.shape[2]
    step = width // CHUNKS
    copies = []
    for i in range(CHUNKS):
        cols = pl.ds(i * step, step)
        copies.append([
            pltpu.make_async_copy(act.at[0, :, cols], rows_v.at[pl.ds(0, tokens), cols], sems.at[i, 0]),
            pltpu.make_async_copy(grad.at[0, :, cols], rows_v.at[pl.ds(tokens, tokens), cols], sems.at[i, 1]),
            pltpu.make_async_copy(proj.at[0, cols, :], proj_v.at[cols, :], sems.at[i, 2]),
        ])
        for c in copies[-1]:
            c.start()
    for c in scalars:
        c.wait()
    half = proj.shape[2] // 2
    seqs = lengths.shape[0]
    slots = tokens // seqs
    pairs = pairing.shape[0]
    place = lax.broadcasted_iota(jnp.int32, (slots, half), 0)
    signs, weights = [], []
    for p in range(pairs):
        chosen, rejected = pairing[p, 0], pairing[p, 1]
        blocks = []
        margin = jnp.float32(0)
        for s in range(seqs):
            coef = jnp.where(rejected == s, 1.0, 0.0) - jnp.where(chosen == s, 1.0, 0.0)
            blocks.append(jnp.where(place < lengths[s], coef, 0.0))
            margin = jnp.where(chosen == s, margin + rewards[s], margin)
        for s in range(seqs):
            margin = jnp.where(rejected == s, margin - rewards[s], margin)
        signs.append(jnp.concatenate(blocks, axis=0))
        weights.append(1.0 - jax.nn.sigmoid(jnp.full((half, half), margin, F32)))
    total = jnp.zeros((2 * tokens, 2 * half), F32)
    for i in range(CHUNKS):
        for c in copies[i]:
            c.wait()
        cols = pl.ds(i * step, step)
        total += jnp.dot(rows_v[:, cols], proj_v[cols, :], preferred_element_type=F32)
    a = total[:tokens, :half]
    g = total[tokens:, half:]
    g = jnp.concatenate([g * s for s in signs], axis=1)
    g_hi = g.astype(BF16)
    g_lo = (g - g_hi.astype(F32)).astype(BF16)
    a_hi = a.astype(BF16)
    a_lo = (a - a_hi.astype(F32)).astype(BF16)

    def over_tokens(l, r):
        return lax.dot_general(l, r, (((0,), (0,)), ((), ())), preferred_element_type=F32)

    t = over_tokens(g_hi, a_hi) + (over_tokens(g_hi, a_lo) + over_tokens(g_lo, a_hi))
    outer[:, :half] = t * jnp.concatenate(weights, axis=0)
    parts = [outer[pl.ds(k, pairs * 8, stride=8), :half] for k in range(8)]
    flat = jnp.concatenate(parts, axis=1).astype(BF16)
    out[...] = flat


def score_kernel(train, queries, out, train_f):
    members = train.shape[0] // 16
    for j in range(4):
        train_f[j] = train[:, 128 * j : 128 * j + 128].astype(F32)
    total = None
    for s in range(8):
        rows = [train_f[j, pl.ds(s, members * 2, stride=8), :].astype(BF16) for j in range(4)]
        rows = jnp.concatenate(rows, axis=1)
        term = lax.dot_general(
            rows, queries[:, pl.ds(512 * s, 512)], (((1,), (1,)), ((), ())), preferred_element_type=F32
        )
        total = term if total is None else total + term
    mine = lax.axis_index("zh") * 2 + lax.axis_index("zm")
    for layer in range(4):
        out[layer] = jnp.where(mine == layer, total, 0.0)


def sum_kernel(got, out):
    for half in range(2):
        total = got[0, half]
        for k in range(1, got.shape[0]):
            total = total + got[k, half]
        out[:, 128 * half : 128 * half + 128] = total


def local(activations, out_grads, projectors, rewards, lengths, pairing, queries):
    tokens, width = activations.shape[1:]
    members = lax.axis_size(PAIR_AXES)
    hbm = pl.BlockSpec(memory_space=pltpu.HBM)
    vmem = pl.BlockSpec(memory_space=pltpu.VMEM)

    train = pl.pallas_call(
        train_kernel,
        out_shape=jax.ShapeDtypeStruct((16, 512), BF16),
        in_specs=[hbm] * 6,
        out_specs=vmem,
        scratch_shapes=[
            pltpu.VMEM((2 * tokens, width), BF16),
            pltpu.VMEM((width, projectors.shape[2]), BF16),
            pltpu.VMEM((projectors.shape[2], projectors.shape[2]), F32),
            pltpu.SMEM(rewards.shape, rewards.dtype),
            pltpu.SMEM(lengths.shape, lengths.dtype),
            pltpu.SMEM(pairing.shape, pairing.dtype),
            pltpu.SemaphoreType.DMA((CHUNKS, 3)),
            pltpu.SemaphoreType.DMA((3,)),
        ],
        compiler_params=pltpu.CompilerParams(vmem_limit_bytes=62200000),
        cost_estimate=pl.CostEstimate(flops=2 * 256 * 5120 * 128, bytes_accessed=4 << 20, transcendentals=0),
        name="train",
    )(activations, out_grads, projectors, rewards, lengths, pairing)
    held = queries[0]
    gathers = list(PAIR_AXES)
    for stage, axes in enumerate(QUERY_AXES):
        copies = jnp.broadcast_to(held, (lax.axis_size(axes),) + held.shape)
        held = lax.all_to_all(copies, axes, 0, 0).reshape(-1, held.shape[1])
        if stage == 0:
            for axis in gathers[:1]:
                train = lax.all_gather(train, axis, axis=0, tiled=True)
            held, train = lax.optimization_barrier((held, train))
    for axis in gathers[1:]:
        train = lax.all_gather(train, axis, axis=0, tiled=True)

    partial = pl.pallas_call(
        score_kernel,
        out_shape=jax.ShapeDtypeStruct((4, members * 2, 128), F32),
        in_specs=[vmem, vmem],
        out_specs=vmem,
        scratch_shapes=[pltpu.VMEM((4, members * 16, 128), F32)],
        compiler_params=pltpu.CompilerParams(vmem_limit_bytes=16 << 20),
        cost_estimate=pl.CostEstimate(flops=2 * 32 * 64 * 4096, bytes_accessed=1 << 20, transcendentals=0),
        name="score",
    )(train, held)
    got = lax.all_to_all(partial.reshape(4 * members, 2, 128), ("layer", "zh", "zm", "zl"), 0, 0)
    return pl.pallas_call(
        sum_kernel,
        out_shape=jax.ShapeDtypeStruct((2, 256), F32),
        in_specs=[vmem],
        out_specs=vmem,
        compiler_params=pltpu.CompilerParams(vmem_limit_bytes=1 << 20),
        name="total",
    )(got.reshape(-1, 2, 2, 128))


def solution(mesh):
    fine = Mesh(mesh.devices.reshape(4, 2, 2, 2, 4, 4), ("layer",) + DP)
    return jax.shard_map(
        local,
        mesh=fine,
        in_specs=(
            P("layer", DP, None),
            P("layer", DP, None),
            P("layer", None, None),
            P(DP),
            P(DP),
            P(DP, None),
            P("layer", DP, None),
        ),
        out_specs=P(DP, "layer"),
        check_vma=False,
    )
```

```python
import jax
import jax.numpy as jnp
from jax import lax
from jax.experimental import pallas as pl
from jax.experimental.pallas import tpu as pltpu
from jax.sharding import Mesh, PartitionSpec as P

DP = ("zh", "zm", "zl", "x", "yh")
PAIR_AXES = ("zm", "zl", "zh")
QUERY_AXES = (("yh",), ("x",))
CHUNKS = 4
F32 = jnp.float32
BF16 = jnp.bfloat16


def train_kernel(
    act, grad, proj, rewards_in, lengths_in, pairing_in, out, rows_v, proj_v, outer, rewards, lengths, pairing, sems, small
):
    given = [(rewards_in, rewards), (lengths_in, lengths), (pairing_in, pairing)]
    scalars = [pltpu.make_async_copy(a, b, small.at[i]) for i, (a, b) in enumerate(given)]
    for c in scalars:
        c.start()
    tokens, width = act.shape[1], act.shape[2]
    step = width // CHUNKS
    copies = []
    for i in range(CHUNKS):
        cols = pl.ds(i * step, step)
        copies.append([
            pltpu.make_async_copy(act.at[0, :, cols], rows_v.at[pl.ds(0, tokens), cols], sems.at[i, 0]),
            pltpu.make_async_copy(grad.at[0, :, cols], rows_v.at[pl.ds(tokens, tokens), cols], sems.at[i, 1]),
            pltpu.make_async_copy(proj.at[0, cols, :], proj_v.at[cols, :], sems.at[i, 2]),
        ])
        for c in copies[-1]:
            c.start()
    for c in scalars:
        c.wait()
    half = proj.shape[2] // 2
    seqs = lengths.shape[0]
    slots = tokens // seqs
    pairs = pairing.shape[0]
    place = lax.broadcasted_iota(jnp.int32, (slots, half), 0)
    signs, weights = [], []
    for p in range(pairs):
        chosen, rejected = pairing[p, 0], pairing[p, 1]
        blocks = []
        margin = jnp.float32(0)
        for s in range(seqs):
            coef = jnp.where(rejected == s, 1.0, 0.0) - jnp.where(chosen == s, 1.0, 0.0)
            blocks.append(jnp.where(place < lengths[s], coef, 0.0))
            margin = jnp.where(chosen == s, margin + rewards[s], margin)
        for s in range(seqs):
            margin = jnp.where(rejected == s, margin - rewards[s], margin)
        signs.append(jnp.concatenate(blocks, axis=0))
        weights.append(1.0 - jax.nn.sigmoid(jnp.full((half, half), margin, F32)))
    total = jnp.zeros((2 * tokens, 2 * half), F32)
    for i in range(CHUNKS):
        for c in copies[i]:
            c.wait()
        cols = pl.ds(i * step, step)
        total += jnp.dot(rows_v[:, cols], proj_v[cols, :], preferred_element_type=F32)
    a = total[:tokens, :half]
    g = total[tokens:, half:]
    g = jnp.concatenate([g * s for s in signs], axis=1)
    g_hi = g.astype(BF16)
    g_lo = (g - g_hi.astype(F32)).astype(BF16)
    a_hi = a.astype(BF16)
    a_lo = (a - a_hi.astype(F32)).astype(BF16)

    def over_tokens(l, r):
        return lax.dot_general(l, r, (((0,), (0,)), ((), ())), preferred_element_type=F32)

    t = over_tokens(g_hi, a_hi) + (over_tokens(g_hi, a_lo) + over_tokens(g_lo, a_hi))
    outer[:, :half] = t * jnp.concatenate(weights, axis=0)
    parts = [outer[pl.ds(k, pairs * 8, stride=8), :half] for k in range(8)]
    flat = jnp.concatenate(parts, axis=1).astype(BF16)
    out[...] = flat


def score_kernel(train, queries, out, train_f):
    members = train.shape[0] // 16
    for j in range(4):
        train_f[j] = train[:, 128 * j : 128 * j + 128].astype(F32)
    total = None
    for s in range(8):
        rows = [train_f[j, pl.ds(s, members * 2, stride=8), :].astype(BF16) for j in range(4)]
        rows = jnp.concatenate(rows, axis=1)
        term = lax.dot_general(
            rows, queries[:, pl.ds(512 * s, 512)], (((1,), (1,)), ((), ())), preferred_element_type=F32
        )
        total = term if total is None else total + term
    mine = lax.axis_index("zh") * 2 + lax.axis_index("zm")
    for layer in range(4):
        out[layer] = jnp.where(mine == layer, total, 0.0)


def sum_kernel(got, out):
    for half in range(2):
        total = None
        for k in range(got.shape[0]):
            for n in range(got.shape[2]):
                total = got[k, half, n] if total is None else total + got[k, half, n]
        out[:, 128 * half : 128 * half + 128] = total


def local(activations, out_grads, projectors, rewards, lengths, pairing, queries):
    tokens, width = activations.shape[1:]
    members = lax.axis_size(PAIR_AXES)
    hbm = pl.BlockSpec(memory_space=pltpu.HBM)
    vmem = pl.BlockSpec(memory_space=pltpu.VMEM)

    train = pl.pallas_call(
        train_kernel,
        out_shape=jax.ShapeDtypeStruct((16, 512), BF16),
        in_specs=[hbm] * 6,
        out_specs=vmem,
        scratch_shapes=[
            pltpu.VMEM((2 * tokens, width), BF16),
            pltpu.VMEM((width, projectors.shape[2]), BF16),
            pltpu.VMEM((projectors.shape[2], projectors.shape[2]), F32),
            pltpu.SMEM(rewards.shape, rewards.dtype),
            pltpu.SMEM(lengths.shape, lengths.dtype),
            pltpu.SMEM(pairing.shape, pairing.dtype),
            pltpu.SemaphoreType.DMA((CHUNKS, 3)),
            pltpu.SemaphoreType.DMA((3,)),
        ],
        compiler_params=pltpu.CompilerParams(vmem_limit_bytes=62200000),
        cost_estimate=pl.CostEstimate(flops=2 * 256 * 5120 * 128, bytes_accessed=4 << 20, transcendentals=0),
        name="train",
    )(activations, out_grads, projectors, rewards, lengths, pairing)
    held = queries[0]
    gathers = list(PAIR_AXES)
    for stage, axes in enumerate(QUERY_AXES):
        copies = jnp.broadcast_to(held, (lax.axis_size(axes),) + held.shape)
        held = lax.all_to_all(copies, axes, 0, 0).reshape(-1, held.shape[1])
        if stage == 0:
            for axis in gathers[:1]:
                train = lax.all_gather(train, axis, axis=0, tiled=True)
            held, train = lax.optimization_barrier((held, train))
    for axis in gathers[1:]:
        train = lax.all_gather(train, axis, axis=0, tiled=True)

    partial = pl.pallas_call(
        score_kernel,
        out_shape=jax.ShapeDtypeStruct((4, members * 2, 128), F32),
        in_specs=[vmem, vmem],
        out_specs=vmem,
        scratch_shapes=[pltpu.VMEM((4, members * 16, 128), F32)],
        compiler_params=pltpu.CompilerParams(vmem_limit_bytes=16 << 20),
        cost_estimate=pl.CostEstimate(flops=2 * 32 * 64 * 4096, bytes_accessed=1 << 20, transcendentals=0),
        name="score",
    )(train, held)
    got = lax.all_to_all(partial.reshape(4 * members, 2, 128), ("layer",) + PAIR_AXES[::-1], 0, 0)
    return pl.pallas_call(
        sum_kernel,
        out_shape=jax.ShapeDtypeStruct((2, 256), F32),
        in_specs=[vmem],
        out_specs=vmem,
        compiler_params=pltpu.CompilerParams(vmem_limit_bytes=1 << 20),
        name="total",
    )(got.reshape(-1, 2, 2, 2, 128))


def solution(mesh):
    fine = Mesh(mesh.devices.reshape(4, 2, 2, 2, 4, 4), ("layer",) + DP)
    return jax.shard_map(
        local,
        mesh=fine,
        in_specs=(
            P("layer", DP, None),
            P("layer", DP, None),
            P("layer", None, None),
            P(DP),
            P(DP),
            P(DP, None),
            P("layer", DP, None),
        ),
        out_specs=P(DP, "layer"),
        check_vma=False,
    )
```

```python
import jax
import jax.numpy as jnp
from jax import lax
from jax.experimental import pallas as pl
from jax.experimental.pallas import tpu as pltpu
from jax.sharding import Mesh, PartitionSpec as P

DP = ("zh", "zm", "zl", "x", "yh")
PAIR_AXES = ("zm", "zl", "zh")
QUERY_AXES = (("yh",), ("x",))
CHUNKS = 4
F32 = jnp.float32
BF16 = jnp.bfloat16


def train_kernel(
    act, grad, proj, rewards_in, lengths_in, pairing_in, out, rows_v, proj_v, outer, rewards, lengths, pairing, sems, small
):
    given = [(rewards_in, rewards), (lengths_in, lengths), (pairing_in, pairing)]
    scalars = [pltpu.make_async_copy(a, b, small.at[i]) for i, (a, b) in enumerate(given)]
    for c in scalars:
        c.start()
    tokens, width = act.shape[1], act.shape[2]
    step = width // CHUNKS
    copies = []
    for i in range(CHUNKS):
        cols = pl.ds(i * step, step)
        copies.append([
            pltpu.make_async_copy(act.at[0, :, cols], rows_v.at[pl.ds(0, tokens), cols], sems.at[i, 0]),
            pltpu.make_async_copy(grad.at[0, :, cols], rows_v.at[pl.ds(tokens, tokens), cols], sems.at[i, 1]),
            pltpu.make_async_copy(proj.at[0, cols, :], proj_v.at[cols, :], sems.at[i, 2]),
        ])
        for c in copies[-1]:
            c.start()
    for c in scalars:
        c.wait()
    half = proj.shape[2] // 2
    seqs = lengths.shape[0]
    slots = tokens // seqs
    pairs = pairing.shape[0]
    place = lax.broadcasted_iota(jnp.int32, (slots, half), 0)
    signs, weights = [], []
    for p in range(pairs):
        chosen, rejected = pairing[p, 0], pairing[p, 1]
        blocks = []
        margin = jnp.float32(0)
        for s in range(seqs):
            coef = jnp.where(rejected == s, 1.0, 0.0) - jnp.where(chosen == s, 1.0, 0.0)
            blocks.append(jnp.where(place < lengths[s], coef, 0.0))
            margin = jnp.where(chosen == s, margin + rewards[s], margin)
        for s in range(seqs):
            margin = jnp.where(rejected == s, margin - rewards[s], margin)
        signs.append(jnp.concatenate(blocks, axis=0))
        weights.append(1.0 - jax.nn.sigmoid(jnp.full((half, half), margin, F32)))
    total = jnp.zeros((2 * tokens, 2 * half), F32)
    for i in range(CHUNKS):
        for c in copies[i]:
            c.wait()
        cols = pl.ds(i * step, step)
        total += jnp.dot(rows_v[:, cols], proj_v[cols, :], preferred_element_type=F32)
    a = total[:tokens, :half]
    g = total[tokens:, half:]
    g = jnp.concatenate([g * s for s in signs], axis=1)
    g_hi = g.astype(BF16)
    g_lo = (g - g_hi.astype(F32)).astype(BF16)
    a_hi = a.astype(BF16)
    a_lo = (a - a_hi.astype(F32)).astype(BF16)

    def over_tokens(l, r):
        return lax.dot_general(l, r, (((0,), (0,)), ((), ())), preferred_element_type=F32)

    t = over_tokens(g_hi, a_hi) + (over_tokens(g_hi, a_lo) + over_tokens(g_lo, a_hi))
    outer[:, :half] = t * jnp.concatenate(weights, axis=0)
    parts = [outer[pl.ds(k, pairs * 8, stride=8), :half] for k in range(8)]
    flat = jnp.concatenate(parts, axis=1).astype(BF16)
    out[...] = flat


def score_kernel(train, queries, out, train_f):
    members = train.shape[0] // 16
    for j in range(4):
        train_f[j] = train[:, 128 * j : 128 * j + 128].astype(F32)
    total = None
    for s in range(8):
        rows = [train_f[j, pl.ds(s, members * 2, stride=8), :].astype(BF16) for j in range(4)]
        rows = jnp.concatenate(rows, axis=1)
        term = lax.dot_general(
            rows, queries[:, pl.ds(512 * s, 512)], (((1,), (1,)), ((), ())), preferred_element_type=F32
        )
        total = term if total is None else total + term
    mine = lax.axis_index("zh") * 2 + lax.axis_index("zm")
    for layer in range(4):
        out[layer] = jnp.where(mine == layer, total, 0.0)


def sum_kernel(got, out):
    for half in range(2):
        total = None
        for k in range(got.shape[0]):
            for n in range(got.shape[2]):
                total = got[k, half, n] if total is None else total + got[k, half, n]
        out[:, 128 * half : 128 * half + 128] = total


def local(activations, out_grads, projectors, rewards, lengths, pairing, queries):
    tokens, width = activations.shape[1:]
    members = lax.axis_size(PAIR_AXES)
    hbm = pl.BlockSpec(memory_space=pltpu.HBM)
    vmem = pl.BlockSpec(memory_space=pltpu.VMEM)

    train = pl.pallas_call(
        train_kernel,
        out_shape=pltpu.VMEM((16, 512), BF16),
        in_specs=[hbm] * 6,
        out_specs=vmem,
        scratch_shapes=[
            pltpu.VMEM((2 * tokens, width), BF16),
            pltpu.VMEM((width, projectors.shape[2]), BF16),
            pltpu.VMEM((projectors.shape[2], projectors.shape[2]), F32),
            pltpu.SMEM(rewards.shape, rewards.dtype),
            pltpu.SMEM(lengths.shape, lengths.dtype),
            pltpu.SMEM(pairing.shape, pairing.dtype),
            pltpu.SemaphoreType.DMA((CHUNKS, 3)),
            pltpu.SemaphoreType.DMA((3,)),
        ],
        compiler_params=pltpu.CompilerParams(vmem_limit_bytes=62200000),
        cost_estimate=pl.CostEstimate(flops=2 * 256 * 5120 * 128, bytes_accessed=4 << 20, transcendentals=0),
        name="train",
    )(activations, out_grads, projectors, rewards, lengths, pairing)
    held = queries[0]
    gathers = list(PAIR_AXES)
    for stage, axes in enumerate(QUERY_AXES):
        copies = jnp.broadcast_to(held, (lax.axis_size(axes),) + held.shape)
        held = lax.all_to_all(copies, axes, 0, 0).reshape(-1, held.shape[1])
        if stage == 0:
            for axis in gathers[:1]:
                train = lax.all_gather(train, axis, axis=0, tiled=True)
            held, train = lax.optimization_barrier((held, train))
    for axis in gathers[1:]:
        train = lax.all_gather(train, axis, axis=0, tiled=True)

    partial = pl.pallas_call(
        score_kernel,
        out_shape=jax.ShapeDtypeStruct((4, members * 2, 128), F32),
        in_specs=[vmem, vmem],
        out_specs=vmem,
        scratch_shapes=[pltpu.VMEM((4, members * 16, 128), F32)],
        compiler_params=pltpu.CompilerParams(vmem_limit_bytes=16 << 20),
        cost_estimate=pl.CostEstimate(flops=2 * 32 * 64 * 4096, bytes_accessed=1 << 20, transcendentals=0),
        name="score",
    )(train, held)
    got = lax.all_to_all(partial.reshape(4 * members, 2, 128), ("layer",) + PAIR_AXES[::-1], 0, 0)
    return pl.pallas_call(
        sum_kernel,
        out_shape=jax.ShapeDtypeStruct((2, 256), F32),
        in_specs=[vmem],
        out_specs=vmem,
        compiler_params=pltpu.CompilerParams(vmem_limit_bytes=1 << 20),
        name="total",
    )(got.reshape(-1, 2, 2, 2, 128))


def solution(mesh):
    fine = Mesh(mesh.devices.reshape(4, 2, 2, 2, 4, 4), ("layer",) + DP)
    return jax.shard_map(
        local,
        mesh=fine,
        in_specs=(
            P("layer", DP, None),
            P("layer", DP, None),
            P("layer", None, None),
            P(DP),
            P(DP),
            P(DP, None),
            P("layer", DP, None),
        ),
        out_specs=P(DP, "layer"),
        check_vma=False,
    )
```

```python
import jax
import jax.numpy as jnp
from jax import lax
from jax.experimental import pallas as pl
from jax.experimental.pallas import tpu as pltpu
from jax.sharding import Mesh, PartitionSpec as P

DP = ("zh", "zm", "zl", "x", "yh")
PAIR_AXES = ("zm", "zl", "zh")
QUERY_AXES = (("yh",), ("x",))
CHUNKS = 4
F32 = jnp.float32
BF16 = jnp.bfloat16


def train_kernel(
    act, grad, proj, rewards_in, lengths_in, pairing_in, out, rows_v, proj_v, outer, rewards, lengths, pairing, sems, small
):
    given = [(rewards_in, rewards), (lengths_in, lengths), (pairing_in, pairing)]
    scalars = [pltpu.make_async_copy(a, b, small.at[i]) for i, (a, b) in enumerate(given)]
    for c in scalars:
        c.start()
    tokens, width = act.shape[1], act.shape[2]
    step = width // CHUNKS
    copies = []
    for i in range(CHUNKS):
        cols = pl.ds(i * step, step)
        copies.append([
            pltpu.make_async_copy(act.at[0, :, cols], rows_v.at[pl.ds(0, tokens), cols], sems.at[i, 0]),
            pltpu.make_async_copy(grad.at[0, :, cols], rows_v.at[pl.ds(tokens, tokens), cols], sems.at[i, 1]),
            pltpu.make_async_copy(proj.at[0, cols, :], proj_v.at[cols, :], sems.at[i, 2]),
        ])
        for c in copies[-1]:
            c.start()
    for c in scalars:
        c.wait()
    half = proj.shape[2] // 2
    seqs = lengths.shape[0]
    slots = tokens // seqs
    pairs = pairing.shape[0]
    place = lax.broadcasted_iota(jnp.int32, (slots, half), 0)
    signs, weights = [], []
    for p in range(pairs):
        chosen, rejected = pairing[p, 0], pairing[p, 1]
        blocks = []
        margin = jnp.float32(0)
        for s in range(seqs):
            coef = jnp.where(rejected == s, 1.0, 0.0) - jnp.where(chosen == s, 1.0, 0.0)
            blocks.append(jnp.where(place < lengths[s], coef, 0.0))
            margin = jnp.where(chosen == s, margin + rewards[s], margin)
        for s in range(seqs):
            margin = jnp.where(rejected == s, margin - rewards[s], margin)
        signs.append(jnp.concatenate(blocks, axis=0))
        weights.append(1.0 - jax.nn.sigmoid(jnp.full((half, half), margin, F32)))
    total = jnp.zeros((2 * tokens, 2 * half), F32)
    for i in range(CHUNKS):
        for c in copies[i]:
            c.wait()
        cols = pl.ds(i * step, step)
        total += jnp.dot(rows_v[:, cols], proj_v[cols, :], preferred_element_type=F32)
    a = total[:tokens, :half]
    g = total[tokens:, half:]
    g = jnp.concatenate([g * s for s in signs], axis=1)
    g_hi = g.astype(BF16)
    g_lo = (g - g_hi.astype(F32)).astype(BF16)
    a_hi = a.astype(BF16)
    a_lo = (a - a_hi.astype(F32)).astype(BF16)

    def over_tokens(l, r):
        return lax.dot_general(l, r, (((0,), (0,)), ((), ())), preferred_element_type=F32)

    t = over_tokens(g_hi, a_hi) + (over_tokens(g_hi, a_lo) + over_tokens(g_lo, a_hi))
    outer[:, :half] = t * jnp.concatenate(weights, axis=0)
    parts = [outer[pl.ds(k, pairs * 8, stride=8), :half] for k in range(8)]
    flat = jnp.concatenate(parts, axis=1).astype(BF16)
    out[...] = flat


def score_kernel(train, queries, out, train_f):
    members = train.shape[0] // 16
    for j in range(4):
        train_f[j] = train[:, 128 * j : 128 * j + 128].astype(F32)
    total = None
    for s in range(8):
        rows = [train_f[j, pl.ds(s, members * 2, stride=8), :].astype(BF16) for j in range(4)]
        rows = jnp.concatenate(rows, axis=1)
        term = lax.dot_general(
            rows, queries[:, pl.ds(512 * s, 512)], (((1,), (1,)), ((), ())), preferred_element_type=F32
        )
        total = term if total is None else total + term
    mine = lax.axis_index("zh") * 2 + lax.axis_index("zm")
    for layer in range(4):
        out[layer] = jnp.where(mine == layer, total, 0.0)


def sum_kernel(got, out):
    for half in range(2):
        total = None
        for k in range(got.shape[0]):
            for n in range(got.shape[2]):
                total = got[k, half, n] if total is None else total + got[k, half, n]
        out[:, 128 * half : 128 * half + 128] = total


def copy_kernel(held, out, sems):
    copies = [pltpu.make_async_copy(held, out.at[n], sems.at[n]) for n in range(out.shape[0])]
    for c in copies:
        c.start()
    for c in copies:
        c.wait()


def local(activations, out_grads, projectors, rewards, lengths, pairing, queries):
    tokens, width = activations.shape[1:]
    members = lax.axis_size(PAIR_AXES)
    hbm = pl.BlockSpec(memory_space=pltpu.HBM)
    vmem = pl.BlockSpec(memory_space=pltpu.VMEM)

    train = pl.pallas_call(
        train_kernel,
        out_shape=pltpu.VMEM((16, 512), BF16),
        in_specs=[hbm] * 6,
        out_specs=vmem,
        scratch_shapes=[
            pltpu.VMEM((2 * tokens, width), BF16),
            pltpu.VMEM((width, projectors.shape[2]), BF16),
            pltpu.VMEM((projectors.shape[2], projectors.shape[2]), F32),
            pltpu.SMEM(rewards.shape, rewards.dtype),
            pltpu.SMEM(lengths.shape, lengths.dtype),
            pltpu.SMEM(pairing.shape, pairing.dtype),
            pltpu.SemaphoreType.DMA((CHUNKS, 3)),
            pltpu.SemaphoreType.DMA((3,)),
        ],
        compiler_params=pltpu.CompilerParams(vmem_limit_bytes=62200000),
        cost_estimate=pl.CostEstimate(flops=2 * 256 * 5120 * 128, bytes_accessed=4 << 20, transcendentals=0),
        name="train",
    )(activations, out_grads, projectors, rewards, lengths, pairing)
    held = queries[0]
    gathers = list(PAIR_AXES)
    for stage, axes in enumerate(QUERY_AXES):
        n = lax.axis_size(axes)
        if stage == 0:
            copies = jnp.broadcast_to(held, (n,) + held.shape)
        else:
            copies = pl.pallas_call(
                copy_kernel,
                out_shape=jax.ShapeDtypeStruct((n,) + held.shape, BF16),
                in_specs=[vmem],
                out_specs=hbm,
                scratch_shapes=[pltpu.SemaphoreType.DMA((n,))],
                compiler_params=pltpu.CompilerParams(vmem_limit_bytes=16 << 20),
                name="copies",
            )(held)
        held = lax.all_to_all(copies, axes, 0, 0).reshape(-1, held.shape[1])
        if stage == 0:
            for axis in gathers[:1]:
                train = lax.all_gather(train, axis, axis=0, tiled=True)
            held, train = lax.optimization_barrier((held, train))
    for axis in gathers[1:]:
        train = lax.all_gather(train, axis, axis=0, tiled=True)

    partial = pl.pallas_call(
        score_kernel,
        out_shape=jax.ShapeDtypeStruct((4, members * 2, 128), F32),
        in_specs=[vmem, vmem],
        out_specs=vmem,
        scratch_shapes=[pltpu.VMEM((4, members * 16, 128), F32)],
        compiler_params=pltpu.CompilerParams(vmem_limit_bytes=16 << 20),
        cost_estimate=pl.CostEstimate(flops=2 * 32 * 64 * 4096, bytes_accessed=1 << 20, transcendentals=0),
        name="score",
    )(train, held)
    got = lax.all_to_all(partial.reshape(4 * members, 2, 128), ("layer",) + PAIR_AXES[::-1], 0, 0)
    return pl.pallas_call(
        sum_kernel,
        out_shape=jax.ShapeDtypeStruct((2, 256), F32),
        in_specs=[vmem],
        out_specs=vmem,
        compiler_params=pltpu.CompilerParams(vmem_limit_bytes=1 << 20),
        name="total",
    )(got.reshape(-1, 2, 2, 2, 128))


def solution(mesh):
    fine = Mesh(mesh.devices.reshape(4, 2, 2, 2, 4, 4), ("layer",) + DP)
    return jax.shard_map(
        local,
        mesh=fine,
        in_specs=(
            P("layer", DP, None),
            P("layer", DP, None),
            P("layer", None, None),
            P(DP),
            P(DP),
            P(DP, None),
            P("layer", DP, None),
        ),
        out_specs=P(DP, "layer"),
        check_vma=False,
    )
```

```python
import jax
import jax.numpy as jnp
from jax import lax
from jax.experimental import pallas as pl
from jax.experimental.pallas import tpu as pltpu
from jax.sharding import Mesh, PartitionSpec as P

DP = ("zh", "zm", "zl", "x", "yh")
PAIR_AXES = ("zm", "zh", "zl")
QUERY_AXES = (("yh",), ("x",))
CHUNKS = 4
F32 = jnp.float32
BF16 = jnp.bfloat16


def train_kernel(
    act, grad, proj, rewards_in, lengths_in, pairing_in, out, rows_v, proj_v, outer, rewards, lengths, pairing, sems, small
):
    given = [(rewards_in, rewards), (lengths_in, lengths), (pairing_in, pairing)]
    scalars = [pltpu.make_async_copy(a, b, small.at[i]) for i, (a, b) in enumerate(given)]
    for c in scalars:
        c.start()
    tokens, width = act.shape[1], act.shape[2]
    step = width // CHUNKS
    copies = []
    for i in range(CHUNKS):
        cols = pl.ds(i * step, step)
        copies.append([
            pltpu.make_async_copy(act.at[0, :, cols], rows_v.at[pl.ds(0, tokens), cols], sems.at[i, 0]),
            pltpu.make_async_copy(grad.at[0, :, cols], rows_v.at[pl.ds(tokens, tokens), cols], sems.at[i, 1]),
            pltpu.make_async_copy(proj.at[0, cols, :], proj_v.at[cols, :], sems.at[i, 2]),
        ])
        for c in copies[-1]:
            c.start()
    for c in scalars:
        c.wait()
    half = proj.shape[2] // 2
    seqs = lengths.shape[0]
    slots = tokens // seqs
    pairs = pairing.shape[0]
    place = lax.broadcasted_iota(jnp.int32, (slots, half), 0)
    signs, weights = [], []
    for p in range(pairs):
        chosen, rejected = pairing[p, 0], pairing[p, 1]
        blocks = []
        margin = jnp.float32(0)
        for s in range(seqs):
            coef = jnp.where(rejected == s, 1.0, 0.0) - jnp.where(chosen == s, 1.0, 0.0)
            blocks.append(jnp.where(place < lengths[s], coef, 0.0))
            margin = jnp.where(chosen == s, margin + rewards[s], margin)
        for s in range(seqs):
            margin = jnp.where(rejected == s, margin - rewards[s], margin)
        signs.append(jnp.concatenate(blocks, axis=0))
        weights.append(1.0 - jax.nn.sigmoid(jnp.full((half, half), margin, F32)))
    total = jnp.zeros((2 * tokens, 2 * half), F32)
    for i in range(CHUNKS):
        for c in copies[i]:
            c.wait()
        cols = pl.ds(i * step, step)
        total += jnp.dot(rows_v[:, cols], proj_v[cols, :], preferred_element_type=F32)
    a = total[:tokens, :half]
    g = total[tokens:, half:]
    g = jnp.concatenate([g * s for s in signs], axis=1)
    g_hi = g.astype(BF16)
    g_lo = (g - g_hi.astype(F32)).astype(BF16)
    a_hi = a.astype(BF16)
    a_lo = (a - a_hi.astype(F32)).astype(BF16)

    def over_tokens(l, r):
        return lax.dot_general(l, r, (((0,), (0,)), ((), ())), preferred_element_type=F32)

    t = over_tokens(g_hi, a_hi) + (over_tokens(g_hi, a_lo) + over_tokens(g_lo, a_hi))
    outer[:, :half] = t * jnp.concatenate(weights, axis=0)
    parts = [outer[pl.ds(k, pairs * 8, stride=8), :half] for k in range(8)]
    flat = jnp.concatenate(parts, axis=1).astype(BF16)
    out[...] = flat


def score_kernel(train, queries, out, train_f):
    members = train.shape[0] // 16
    for j in range(4):
        train_f[j] = train[:, 128 * j : 128 * j + 128].astype(F32)
    total = None
    for s in range(8):
        rows = [train_f[j, pl.ds(s, members * 2, stride=8), :].astype(BF16) for j in range(4)]
        rows = jnp.concatenate(rows, axis=1)
        term = lax.dot_general(
            rows, queries[:, pl.ds(512 * s, 512)], (((1,), (1,)), ((), ())), preferred_element_type=F32
        )
        total = term if total is None else total + term
    mine = lax.axis_index("zh") * 2 + lax.axis_index("zm")
    for layer in range(4):
        out[layer] = jnp.where(mine == layer, total, 0.0)


def sum_kernel(got, out):
    for half in range(2):
        total = None
        for k in range(got.shape[0]):
            for n in range(got.shape[2]):
                total = got[k, half, n] if total is None else total + got[k, half, n]
        out[:, 128 * half : 128 * half + 128] = total


def local(activations, out_grads, projectors, rewards, lengths, pairing, queries):
    tokens, width = activations.shape[1:]
    members = lax.axis_size(PAIR_AXES)
    hbm = pl.BlockSpec(memory_space=pltpu.HBM)
    vmem = pl.BlockSpec(memory_space=pltpu.VMEM)

    train = pl.pallas_call(
        train_kernel,
        out_shape=pltpu.VMEM((16, 512), BF16),
        in_specs=[hbm] * 6,
        out_specs=vmem,
        scratch_shapes=[
            pltpu.VMEM((2 * tokens, width), BF16),
            pltpu.VMEM((width, projectors.shape[2]), BF16),
            pltpu.VMEM((projectors.shape[2], projectors.shape[2]), F32),
            pltpu.SMEM(rewards.shape, rewards.dtype),
            pltpu.SMEM(lengths.shape, lengths.dtype),
            pltpu.SMEM(pairing.shape, pairing.dtype),
            pltpu.SemaphoreType.DMA((CHUNKS, 3)),
            pltpu.SemaphoreType.DMA((3,)),
        ],
        compiler_params=pltpu.CompilerParams(vmem_limit_bytes=62200000),
        cost_estimate=pl.CostEstimate(flops=2 * 256 * 5120 * 128, bytes_accessed=4 << 20, transcendentals=0),
        name="train",
    )(activations, out_grads, projectors, rewards, lengths, pairing)
    held = queries[0]
    gathers = list(PAIR_AXES)
    for stage, axes in enumerate(QUERY_AXES):
        copies = jnp.broadcast_to(held, (lax.axis_size(axes),) + held.shape)
        held = lax.all_to_all(copies, axes, 0, 0).reshape(-1, held.shape[1])
        if stage == 0:
            for axis in gathers[:1]:
                train = lax.all_gather(train, axis, axis=0, tiled=True)
            held, train = lax.optimization_barrier((held, train))
    for axis in gathers[1:]:
        train = lax.all_gather(train, axis, axis=0, tiled=True)

    partial = pl.pallas_call(
        score_kernel,
        out_shape=jax.ShapeDtypeStruct((4, members * 2, 128), F32),
        in_specs=[vmem, vmem],
        out_specs=vmem,
        scratch_shapes=[pltpu.VMEM((4, members * 16, 128), F32)],
        compiler_params=pltpu.CompilerParams(vmem_limit_bytes=16 << 20),
        cost_estimate=pl.CostEstimate(flops=2 * 32 * 64 * 4096, bytes_accessed=1 << 20, transcendentals=0),
        name="score",
    )(train, held)
    got = lax.all_to_all(partial.reshape(4 * members, 2, 128), ("layer",) + PAIR_AXES[::-1], 0, 0)
    return pl.pallas_call(
        sum_kernel,
        out_shape=jax.ShapeDtypeStruct((2, 256), F32),
        in_specs=[vmem],
        out_specs=vmem,
        compiler_params=pltpu.CompilerParams(vmem_limit_bytes=1 << 20),
        name="total",
    )(got.reshape(4, 2, -1, 2, 128))


def solution(mesh):
    fine = Mesh(mesh.devices.reshape(4, 2, 2, 2, 4, 4), ("layer",) + DP)
    return jax.shard_map(
        local,
        mesh=fine,
        in_specs=(
            P("layer", DP, None),
            P("layer", DP, None),
            P("layer", None, None),
            P(DP),
            P(DP),
            P(DP, None),
            P("layer", DP, None),
        ),
        out_specs=P(DP, "layer"),
        check_vma=False,
    )
```
